256 devices in a mesh: dp: 64 (over x, z, core), feat: 4 (over y).
Axes of the slice: x: 4, y: 4, z: 8, core: 2. Of those that a mesh axis runs over, the one named last changes fastest.
Arguments:
- training_grads: bfloat16 [65536, 8192], P('dp', 'feat'), may hold values from -6 to 6
- validation_grads: bfloat16 [1024, 8192], P('dp', 'feat'), may hold values from -6 to 6
- test_matrix: bfloat16 [65536, 256], P('dp'), may hold values from -0.0234375 to 0.0234375
Outputs:
- scores: float32 [1024, 65536], P(None, ('dp', 'feat'))
The draws below stay inside these ranges and needn't reach their ends.
All inputs are finite; a program needn't handle non-finite values.
Results may differ from the reference program's by a relative error of at most 0.0038.
Values may be sent and summed in bfloat16 or wider, within the bound.
No kernel may reach another device: no remote copies, remote signals or barrier semaphores. Data moves between devices by JAX's collectives and lax.ppermute only.
A program may use at most 64 MiB of HBM per device.

```python
import math
import jax
import jax.numpy as jnp
from jax import lax

WIDTH = 8192
RANK = 256
NTRAIN = 65536
NVAL = 1024


def block_levels(key, shape, split, least, largest):
    gain, own = 1.0, jax.random.fold_in(key, 6)
    for dim, parts in split:
        heights = jnp.exp(jax.random.uniform(jax.random.fold_in(own, dim), (parts,), jnp.float32, least / len(split), largest / len(split)))
        gain = gain * jnp.repeat(heights, shape[dim] // parts).reshape([-1 if axis == dim else 1 for axis in range(len(shape))])
    return gain


def normal_values(stream_key, dims, spread, limit, cuts=(), kind=jnp.bfloat16):
    level = block_levels(stream_key, dims, cuts, -0.22, 0.18) if cuts else 1.0
    entries = jax.random.normal(stream_key, dims, jnp.float32) * spread * level
    return jnp.minimum(jnp.maximum(entries, -limit), limit).astype(kind)


def setup_inputs(seed: int = 0) -> dict:
    key_list = jax.random.split(jax.random.key(seed), 4)
    training_grads = normal_values(key_list[0], (NTRAIN, WIDTH), 1.0, 6.0, ((0, 64), (1, 4)))
    validation_grads = normal_values(key_list[1], (NVAL, WIDTH), 1.0, 6.0, ((0, 64), (1, 4)))
    test_matrix = normal_values(key_list[2], (NTRAIN, RANK), NTRAIN ** -0.5, 0.0234375, ((0, 64),))
    return {"training_grads": training_grads, "validation_grads": validation_grads, "test_matrix": test_matrix}


damping = 0.1

def reference(training_grads, validation_grads, test_matrix):
    highest = lax.Precision.HIGHEST
    basis_raw = jnp.dot(training_grads.T.astype(jnp.float32), test_matrix.astype(jnp.float32), preferred_element_type=jnp.float32)
    basis_gram = jnp.dot(basis_raw.T, basis_raw, precision=highest)
    factor = jnp.linalg.cholesky(basis_gram)
    basis = jax.scipy.linalg.solve_triangular(factor, basis_raw.T, lower=True).T.astype(jnp.bfloat16)
    train_coords = jnp.dot(training_grads.astype(jnp.float32), basis.astype(jnp.float32), preferred_element_type=jnp.float32)
    val_coords = jnp.dot(validation_grads.astype(jnp.float32), basis.astype(jnp.float32), preferred_element_type=jnp.float32)
    curvature = jnp.dot(train_coords.T, train_coords, precision=highest) / NTRAIN
    curvature = curvature + damping * jnp.eye(RANK, dtype=jnp.float32)
    curv_factor = jnp.linalg.cholesky(curvature)
    solved = jax.scipy.linalg.cho_solve((curv_factor, True), val_coords.T)
    return jnp.dot(solved.T, train_coords.T, precision=highest) / math.sqrt(RANK)
```

```python
import math

import jax
import jax.numpy as jnp
from jax import lax
from jax.sharding import Mesh, PartitionSpec as P

damping = 0.1
f32 = jnp.float32


def scatter_sum(value, axis, size):
    rows = value.shape[0] // size
    parts = lax.all_to_all(value, axis, 0, 0, tiled=True)
    return jnp.sum(parts.reshape(size, rows, value.shape[1]), axis=0)


def gather(value, axis, size):
    copies = jnp.broadcast_to(value[None], (size,) + value.shape)
    rows = copies.reshape(size * value.shape[0], value.shape[1])
    return lax.all_to_all(rows, axis, 0, 0, tiled=True)


def local(sizes, training_grads, validation_grads, test_matrix):
    highest = lax.Precision.HIGHEST
    every = ("x", "z", "c", "y")
    devices = math.prod(sizes.values())
    row_count = training_grads.shape[0]
    rank_size = test_matrix.shape[1]
    total_train = row_count * devices // sizes["y"]
    with jax.named_scope("val_gather"):
        val_block = lax.all_gather(validation_grads, ("x", "z", "c"), axis=0, tiled=True)
    with jax.named_scope("raw_basis"):
        partial_basis = lax.dot_general(
            training_grads, test_matrix, (((0,), (0,)), ((), ())), preferred_element_type=f32
        )
        basis_rows = partial_basis
        for axis in ("c", "x", "z"):
            basis_rows = scatter_sum(basis_rows, axis, sizes[axis])
        basis = basis_rows.astype(jnp.bfloat16)
        for axis in ("z", "x", "c"):
            basis = gather(basis, axis, sizes[axis])
    with jax.named_scope("coords"):
        val_part = jnp.dot(val_block, basis, preferred_element_type=f32)
        val_coords = lax.psum(val_part, "y")
        train_part = jnp.dot(training_grads, basis, preferred_element_type=f32)
        mine = scatter_sum(train_part, "y", sizes["y"])
    with jax.named_scope("curvature"):
        stacked = jnp.concatenate(
            [mine * (1.0 / math.sqrt(total_train)), basis_rows * math.sqrt(damping)], axis=0
        )
        part = lax.dot_general(
            stacked, stacked, (((0,), (0,)), ((), ())), precision=highest, preferred_element_type=f32
        )
        part = part.reshape(devices, 2, 128)
        parts = lax.all_to_all(part, every, 0, 0, tiled=True)
        row = jnp.sum(parts, axis=0)
        copies = jnp.broadcast_to(row[None], (devices, 2, 128))
        curvature = lax.all_to_all(copies, every, 0, 0, tiled=True).reshape(rank_size, rank_size)
    with jax.named_scope("solve"):
        curv_factor = jnp.linalg.cholesky(curvature)
        solved = jax.scipy.linalg.cho_solve((curv_factor, True), mine.T)
    return jnp.dot(val_coords, solved, precision=highest) / math.sqrt(rank_size)


def solution(mesh):
    sizes = {"x": 4, "z": 8, "c": 2, "y": 4}
    split = Mesh(mesh.devices.reshape(tuple(sizes.values())), tuple(sizes))
    dp = ("x", "z", "c")

    def run(training_grads, validation_grads, test_matrix):
        return jax.shard_map(
            lambda *args: local(sizes, *args),
            mesh=split,
            in_specs=(P(dp, "y"), P(dp, "y"), P(dp, None)),
            out_specs=P(None, dp + ("y",)),
            check_vma=False,
        )(training_grads, validation_grads, test_matrix)

    return run
```

```python
import functools
import math

import jax
import jax.numpy as jnp
from jax import lax
from jax.experimental import pallas as pl
from jax.experimental.pallas import tpu as pltpu
from jax.sharding import Mesh, PartitionSpec as P

damping = 0.1
f32 = jnp.float32
highest = lax.Precision.HIGHEST
PIVOTS = 4
BAND = 64


def inverse_of_four(k):
    a, b, c = k[0][0], k[0][1], k[1][1]
    ra = 1.0 / (a * c - b * b)
    p, q, r = c * ra, -b * ra, a * ra
    e, f, g, h = k[0][2], k[0][3], k[1][2], k[1][3]
    y00, y01 = p * e + q * g, p * f + q * h
    y10, y11 = q * e + r * g, q * f + r * h
    s00 = k[2][2] - (e * y00 + g * y10)
    s01 = k[2][3] - (e * y01 + g * y11)
    s11 = k[3][3] - (f * y01 + h * y11)
    rs = 1.0 / (s00 * s11 - s01 * s01)
    u, v, w = s11 * rs, -s01 * rs, s00 * rs
    z00, z01 = y00 * u + y01 * v, y00 * v + y01 * w
    z10, z11 = y10 * u + y11 * v, y10 * v + y11 * w
    i00 = p + z00 * y00 + z01 * y01
    i01 = q + z00 * y10 + z01 * y11
    i11 = r + z10 * y10 + z11 * y11
    return [
        [i00, i01, -z00, -z01],
        [i01, i11, -z10, -z11],
        [-z00, -z10, u, v],
        [-z01, -z11, v, w],
    ]


def solve_body(m_ref, x_ref, o_ref, e_ref, *, scale):
    n = m_ref.shape[0]
    rows = lax.broadcasted_iota(jnp.int32, (n, n), 0)
    cols = lax.broadcasted_iota(jnp.int32, (n, n), 1)
    m = m_ref[...]
    diagonal = jnp.where(rows == cols, m, 0.0)
    along = lax.rsqrt(jnp.sum(diagonal, axis=0, keepdims=True))
    down = lax.rsqrt(jnp.sum(diagonal, axis=1, keepdims=True))
    e_ref[:, :n] = m * along * down
    e_ref[:, n:] = x_ref[...].T * down
    tiles = BAND // 8
    chunks = 2 * n // 128
    sub = lax.broadcasted_iota(jnp.int32, (8, 128), 0)
    band_row = lax.broadcasted_iota(jnp.int32, (n, BAND), 0)
    for lo in range(0, n, BAND):
        first = lo // 128
        panel = {
            c: e_ref[lo : lo + BAND, c * 128 : (c + 1) * 128].reshape(tiles, 8, 128)
            for c in range(first, chunks)
        }
        for g in range(0, BAND, PIVOTS):
            tile, s = g // 8, g % 8
            d, lane = (lo + g) // 128, (lo + g) % 128
            column = [
                jnp.broadcast_to(panel[d][:, :, lane + a : lane + a + 1], (tiles, 8, 128))
                for a in range(PIVOTS)
            ]
            block = [
                [
                    jnp.broadcast_to(column[b][tile, s + a : s + a + 1, :], (8, 128))
                    for b in range(PIVOTS)
                ]
                for a in range(PIVOTS)
            ]
            inv = inverse_of_four(block)
            for c in range(d, chunks):
                old = [
                    jnp.broadcast_to(panel[c][tile, s + a : s + a + 1, :], (8, 128))
                    for a in range(PIVOTS)
                ]
                new = [sum(inv[a][b] * old[b] for b in range(PIVOTS)) for a in range(PIVOTS)]
                out = []
                for t in range(tiles):
                    value = panel[c][t] - sum(column[a][t] * new[a] for a in range(PIVOTS))
                    if t == tile:
                        for a in range(PIVOTS):
                            value = jnp.where(sub == s + a, new[a], value)
                    out.append(value)
                panel[c] = jnp.stack(out, axis=0)
        wide = jnp.concatenate(
            [panel[c].reshape(BAND, 128) for c in range(first, chunks)], axis=1
        )
        left = e_ref[:, lo : lo + BAND]
        left = jnp.where((band_row >= lo) & (band_row < lo + BAND), 0.0, left)
        e_ref[:, first * 128 :] = e_ref[:, first * 128 :] - jnp.dot(
            left, wide, precision=highest, preferred_element_type=f32
        )
        e_ref[lo : lo + BAND, first * 128 :] = wide
    o_ref[...] = e_ref[:, n:] * (down * scale)


def solve(m, x, scale):
    n = m.shape[0]
    return pl.pallas_call(
        functools.partial(solve_body, scale=scale),
        out_shape=jax.ShapeDtypeStruct((n, n), f32),
        in_specs=[pl.BlockSpec(memory_space=pltpu.VMEM)] * 2,
        out_specs=pl.BlockSpec(memory_space=pltpu.VMEM),
        scratch_shapes=[pltpu.VMEM((n, 2 * n), f32)],
        compiler_params=pltpu.CompilerParams(vmem_limit_bytes=16 * 2**20),
        cost_estimate=pl.CostEstimate(
            flops=4 * n**3, bytes_accessed=12 * n * n, transcendentals=n * n
        ),
        name="solve",
    )(m, x)


def members(sizes, axes):
    return math.prod(sizes[a] for a in axes)


def scatter_sum(sizes, value, axes):
    n = members(sizes, axes)
    parts = lax.all_to_all(value, axes, 0, 0, tiled=True)
    return jnp.sum(parts.reshape((n, value.shape[0] // n) + value.shape[1:]), axis=0)


def gather(sizes, value, axes):
    n = members(sizes, axes)
    copies = jnp.broadcast_to(value[None], (n,) + value.shape)
    rows = copies.reshape((n * value.shape[0],) + value.shape[1:])
    return lax.all_to_all(rows, axes, 0, 0, tiled=True)


def local(sizes, training_grads, validation_grads, test_matrix):
    row_count = training_grads.shape[0]
    val_rows = validation_grads.shape[0]
    rank_size = test_matrix.shape[1]
    total_train = row_count * members(sizes, ("x", "z", "c"))
    planes = members(sizes, ("x", "z"))
    with jax.named_scope("val_gather"):
        val_block = lax.all_gather(validation_grads, ("x", "z"), axis=0, tiled=True)
    with jax.named_scope("raw_basis"):
        basis_rows = lax.dot_general(
            training_grads, test_matrix, (((0,), (0,)), ((), ())), preferred_element_type=f32
        )
        for axis in ("c", "x", "z"):
            basis_rows = scatter_sum(sizes, basis_rows, (axis,))
        basis = basis_rows.astype(jnp.bfloat16)
        basis = gather(sizes, basis, ("x", "z"))
        basis = gather(sizes, basis, ("c",))
    with jax.named_scope("coords"):
        val_part = jnp.dot(val_block, basis, preferred_element_type=f32)
        train_part = jnp.dot(training_grads, basis, preferred_element_type=f32)
        train_part, val_part = lax.optimization_barrier((train_part, val_part))
        val_half = lax.psum(val_part, "y")
        mine = scatter_sum(sizes, train_part, ("y",))
    with jax.named_scope("curvature"):
        first = (((0,), (0,)), ((), ()))
        part = lax.dot_general(mine, mine, first, precision=highest) / total_train
        part = part + damping * lax.dot_general(basis_rows, basis_rows, first, precision=highest)
        part = scatter_sum(sizes, part, ("z", "c"))
        part = jnp.sum(gather(sizes, part, ("x", "y")).reshape((-1,) + part.shape), axis=0)
        curvature = gather(sizes, part, ("z", "c"))
    with jax.named_scope("solve"):
        solved = solve(curvature, mine, 1.0 / math.sqrt(rank_size))
    with jax.named_scope("scores"):
        swap = [(0, 1), (1, 0)]
        other = lax.ppermute(val_half, "c", swap)
        even = lax.axis_index("c") == 0
        halves = [jnp.where(even, val_half, other), jnp.where(even, other, val_half)]
        halves = [h.reshape(planes, val_rows, rank_size) for h in halves]
        val_coords = jnp.stack(halves, axis=1).reshape(planes * 2 * val_rows, rank_size)
        return jnp.dot(val_coords, solved, precision=lax.Precision.HIGH)


def solution(mesh):
    sizes = {"x": 4, "z": 8, "c": 2, "y": 4}
    split = Mesh(mesh.devices.reshape(tuple(sizes.values())), tuple(sizes))
    dp = ("x", "z", "c")

    def run(training_grads, validation_grads, test_matrix):
        return jax.shard_map(
            functools.partial(local, sizes),
            mesh=split,
            in_specs=(P(dp, "y"), P(dp, "y"), P(dp, None)),
            out_specs=P(None, dp + ("y",)),
            check_vma=False,
        )(training_grads, validation_grads, test_matrix)

    return run
```

```python
import functools
import math

import jax
import jax.numpy as jnp
from jax import lax
from jax.experimental import pallas as pl
from jax.experimental.pallas import tpu as pltpu
from jax.sharding import Mesh, PartitionSpec as P

damping = 0.1
f32 = jnp.float32
highest = lax.Precision.HIGHEST
PIVOTS = 4
BAND = 64


def inverse_of_four(k):
    a, b, c = k[0][0], k[0][1], k[1][1]
    ra = 1.0 / (a * c - b * b)
    p, q, r = c * ra, -b * ra, a * ra
    e, f, g, h = k[0][2], k[0][3], k[1][2], k[1][3]
    y00, y01 = p * e + q * g, p * f + q * h
    y10, y11 = q * e + r * g, q * f + r * h
    s00 = k[2][2] - (e * y00 + g * y10)
    s01 = k[2][3] - (e * y01 + g * y11)
    s11 = k[3][3] - (f * y01 + h * y11)
    rs = 1.0 / (s00 * s11 - s01 * s01)
    u, v, w = s11 * rs, -s01 * rs, s00 * rs
    z00, z01 = y00 * u + y01 * v, y00 * v + y01 * w
    z10, z11 = y10 * u + y11 * v, y10 * v + y11 * w
    i00 = p + z00 * y00 + z01 * y01
    i01 = q + z00 * y10 + z01 * y11
    i11 = r + z10 * y10 + z11 * y11
    return [
        [i00, i01, -z00, -z01],
        [i01, i11, -z10, -z11],
        [-z00, -z10, u, v],
        [-z01, -z11, v, w],
    ]


def solve_body(m_ref, x_ref, o_ref, e_ref, *, scale):
    n = m_ref.shape[0]
    rows = lax.broadcasted_iota(jnp.int32, (n, n), 0)
    cols = lax.broadcasted_iota(jnp.int32, (n, n), 1)
    m = m_ref[...]
    diagonal = jnp.where(rows == cols, m, 0.0)
    along = lax.rsqrt(jnp.sum(diagonal, axis=0, keepdims=True))
    down = lax.rsqrt(jnp.sum(diagonal, axis=1, keepdims=True))
    e_ref[:, :n] = m * along * down
    e_ref[:, n:] = x_ref[...].T * down
    tiles = BAND // 8
    chunks = 2 * n // 128
    sub = lax.broadcasted_iota(jnp.int32, (8, 128), 0)
    band_row = lax.broadcasted_iota(jnp.int32, (n, BAND), 0)
    for lo in range(0, n, BAND):
        first = lo // 128
        panel = {
            c: e_ref[lo : lo + BAND, c * 128 : (c + 1) * 128].reshape(tiles, 8, 128)
            for c in range(first, chunks)
        }
        for g in range(0, BAND, PIVOTS):
            tile, s = g // 8, g % 8
            d, lane = (lo + g) // 128, (lo + g) % 128
            column = [
                jnp.broadcast_to(panel[d][:, :, lane + a : lane + a + 1], (tiles, 8, 128))
                for a in range(PIVOTS)
            ]
            block = [
                [
                    jnp.broadcast_to(column[b][tile, s + a : s + a + 1, :], (8, 128))
                    for b in range(PIVOTS)
                ]
                for a in range(PIVOTS)
            ]
            inv = inverse_of_four(block)
            for c in range(d, chunks):
                old = [
                    jnp.broadcast_to(panel[c][tile, s + a : s + a + 1, :], (8, 128))
                    for a in range(PIVOTS)
                ]
                new = [sum(inv[a][b] * old[b] for b in range(PIVOTS)) for a in range(PIVOTS)]
                out = []
                for t in range(tiles):
                    value = panel[c][t] - sum(column[a][t] * new[a] for a in range(PIVOTS))
                    if t == tile:
                        for a in range(PIVOTS):
                            value = jnp.where(sub == s + a, new[a], value)
                    out.append(value)
                panel[c] = jnp.stack(out, axis=0)
        wide = jnp.concatenate(
            [panel[c].reshape(BAND, 128) for c in range(first, chunks)], axis=1
        )
        left = e_ref[:, lo : lo + BAND]
        left = jnp.where((band_row >= lo) & (band_row < lo + BAND), 0.0, left)
        e_ref[:, first * 128 :] = e_ref[:, first * 128 :] - jnp.dot(
            left, wide, precision=highest, preferred_element_type=f32
        )
        e_ref[lo : lo + BAND, first * 128 :] = wide
    o_ref[...] = e_ref[:, n:] * (down * scale)


def solve(m, x, scale):
    n = m.shape[0]
    return pl.pallas_call(
        functools.partial(solve_body, scale=scale),
        out_shape=jax.ShapeDtypeStruct((n, n), f32),
        in_specs=[pl.BlockSpec(memory_space=pltpu.VMEM)] * 2,
        out_specs=pl.BlockSpec(memory_space=pltpu.VMEM),
        scratch_shapes=[pltpu.VMEM((n, 2 * n), f32)],
        compiler_params=pltpu.CompilerParams(vmem_limit_bytes=16 * 2**20),
        cost_estimate=pl.CostEstimate(
            flops=4 * n**3, bytes_accessed=12 * n * n, transcendentals=n * n
        ),
        name="solve",
    )(m, x)


def members(sizes, axes):
    return math.prod(sizes[a] for a in axes)


def scatter_sum(sizes, value, axes):
    n = members(sizes, axes)
    parts = lax.all_to_all(value, axes, 0, 0, tiled=True)
    return jnp.sum(parts.reshape((n, value.shape[0] // n) + value.shape[1:]), axis=0)


def gather(sizes, value, axes):
    n = members(sizes, axes)
    copies = jnp.broadcast_to(value[None], (n,) + value.shape)
    rows = copies.reshape((n * value.shape[0],) + value.shape[1:])
    return lax.all_to_all(rows, axes, 0, 0, tiled=True)


def local(sizes, training_grads, validation_grads, test_matrix):
    row_count = training_grads.shape[0]
    val_rows = validation_grads.shape[0]
    rank_size = test_matrix.shape[1]
    total_train = row_count * members(sizes, ("x", "z", "c"))
    planes = members(sizes, ("x", "z"))
    feats = sizes["y"]
    quarter = row_count // feats
    val_share = val_rows // feats
    with jax.named_scope("raw_basis"):
        basis_rows = lax.dot_general(
            training_grads, test_matrix, (((0,), (0,)), ((), ())), preferred_element_type=f32
        )
        for axis in ("c", "x", "z"):
            basis_rows = scatter_sum(sizes, basis_rows, (axis,))
        basis = basis_rows.astype(jnp.bfloat16)
        basis = gather(sizes, basis, ("x", "z"))
        basis = gather(sizes, basis, ("c",))
    with jax.named_scope("coords"):
        train_part = jnp.dot(training_grads, basis, preferred_element_type=f32)
        val_part = jnp.dot(validation_grads, basis, preferred_element_type=f32)
        both = jnp.concatenate(
            [
                train_part.reshape(feats, quarter, rank_size),
                val_part.reshape(feats, val_share, rank_size),
                jnp.zeros((feats, 8 - val_share, rank_size), f32),
            ],
            axis=1,
        )
        both = jnp.sum(lax.all_to_all(both, "y", 0, 0, tiled=True), axis=0)
        mine, val_mine = both[:quarter], both[quarter : quarter + val_share]
    with jax.named_scope("curvature"):
        first = (((0,), (0,)), ((), ()))
        part = lax.dot_general(mine, mine, first, precision=highest) / total_train
        part = part + damping * lax.dot_general(basis_rows, basis_rows, first, precision=highest)
        zc = members(sizes, ("z", "c"))
        xy = members(sizes, ("x", "y"))
        share = rank_size // zc
        halves = jnp.broadcast_to(
            val_mine.reshape(1, 2, val_share // 2, rank_size),
            (sizes["z"], 2, val_share // 2, rank_size),
        ).reshape(zc, val_share // 2, rank_size)
        send = jnp.concatenate(
            [
                part.reshape(zc, share, rank_size),
                halves,
                jnp.zeros((zc, 8 - val_share // 2, rank_size), f32),
            ],
            axis=1,
        )
        got = lax.all_to_all(send, ("z", "c"), 0, 0, tiled=True)
        part = jnp.sum(got[:, :share], axis=0)
        val_held = got[:, share : share + val_share // 2].reshape(zc * val_share // 2, rank_size)
        send = jnp.concatenate([part, val_held], axis=0)
        send = jnp.broadcast_to(send[None], (xy,) + send.shape)
        got = lax.all_to_all(send, ("x", "y"), 0, 0, tiled=True)
        part = jnp.sum(got[:, :share], axis=0)
        val_half = got[:, share:].reshape(
            sizes["x"], feats, sizes["z"], 2, 1, val_share // 2, rank_size
        )
        curvature = gather(sizes, part, ("z", "c"))
    with jax.named_scope("solve"):
        other = lax.ppermute(val_half, "c", [(0, 1), (1, 0)])
        solved = solve(curvature, mine, 1.0 / math.sqrt(rank_size))
    with jax.named_scope("scores"):
        even = lax.axis_index("c") == 0
        pair = [jnp.where(even, val_half, other), jnp.where(even, other, val_half)]
        val_coords = jnp.concatenate(pair, axis=4).transpose(0, 2, 3, 1, 4, 5, 6)
        val_coords = val_coords.reshape(planes * 2 * val_rows, rank_size)
        return jnp.dot(val_coords, solved, precision=lax.Precision.HIGH)


def solution(mesh):
    sizes = {"x": 4, "z": 8, "c": 2, "y": 4}
    split = Mesh(mesh.devices.reshape(tuple(sizes.values())), tuple(sizes))
    dp = ("x", "z", "c")

    def run(training_grads, validation_grads, test_matrix):
        return jax.shard_map(
            functools.partial(local, sizes),
            mesh=split,
            in_specs=(P(dp, "y"), P(dp, "y"), P(dp, None)),
            out_specs=P(None, dp + ("y",)),
            check_vma=False,
        )(training_grads, validation_grads, test_matrix)

    return run
```
